32 devices in a mesh: state: 2 (over x), mode: 16 (over z, y, core).
Axes of the slice: x: 2, y: 2, z: 4, core: 2. Of those that a mesh axis runs over, the one named last changes fastest.
Arguments:
- core: bfloat16 [2, 512, 512, 256], P('state', 'mode'), may hold values from -6 to 6
- op_one: bfloat16 [2, 3, 512, 512], replicated, may hold values from -0.25 to 0.25
- op_two: bfloat16 [2, 3, 512, 512], replicated, may hold values from -0.25 to 0.25
- op_three: bfloat16 [2, 3, 256, 256], replicated, may hold values from -0.375 to 0.375
Outputs:
- relaxed: float32 [2, 512, 512, 256], P('state', 'mode')
The draws below stay inside these ranges and needn't reach their ends.
All inputs are finite; a program needn't handle non-finite values.
Results may differ from the reference program's by a relative error of at most 0.0033.
Values may be sent and summed in bfloat16 or wider, within the bound.
A program may use at most 192 MiB of HBM per device.

```python
import jax
import jax.numpy as jnp
from jax import lax

N1 = 512
N2 = 512
N3 = 256
TERMS = 3
N_STATE = 2


def shard_levels(rng, extent, shards, least, top_value):
    gain, own = 1.0, jax.random.fold_in(rng, 6)
    for dim, shards_of in shards:
        heights = jnp.exp(jax.random.uniform(jax.random.fold_in(own, dim), (shards_of,), jnp.float32, least / len(shards), top_value / len(shards)))
        gain = gain * jnp.repeat(heights, extent[dim] // shards_of).reshape([-1 if axis == dim else 1 for axis in range(len(extent))])
    return gain


def gaussian(stream_key, shape, deviation, limit, shards=(), held_as=jnp.bfloat16):
    entries = jax.random.normal(stream_key, shape, jnp.float32) * deviation
    if len(shards) > 0:
        entries = shard_levels(stream_key, shape, shards, -0.22, 0.18) * entries
    return jnp.clip(entries, min=-limit, max=limit).astype(held_as)


def setup_inputs(seed: int = 0) -> dict:
    arg_keys = jax.random.split(jax.random.key(seed), 5)
    return {
        "core": gaussian(arg_keys[0], (N_STATE, N1, N2, N3), 1.0, 6.0, ((0, 2), (1, 16))),
        "op_one": gaussian(arg_keys[1], (N_STATE, TERMS, N1, N1), N1 ** -0.5, 0.25),
        "op_two": gaussian(arg_keys[2], (N_STATE, TERMS, N2, N2), N2 ** -0.5, 0.25),
        "op_three": gaussian(arg_keys[3], (N_STATE, TERMS, N3, N3), N3 ** -0.5, 0.375),
    }


def apply_term(block, first, second, third):
    inner = jnp.einsum("ijk,lk->ijl", block.astype(jnp.float32), third.astype(jnp.float32)).astype(jnp.bfloat16)
    inner = lax.optimization_barrier(inner)
    prepared = jnp.einsum("ab,ibk->iak", second.astype(jnp.float32), inner.astype(jnp.float32)).astype(jnp.bfloat16)
    prepared = lax.optimization_barrier(prepared)
    return jnp.einsum("ab,bjk->ajk", first.astype(jnp.float32), prepared.astype(jnp.float32))


def reference(core, op_one, op_two, op_three):
    diagonal_parts = []
    coupling_parts = []
    for state_number in range(N_STATE):
        block = core[state_number]
        diagonal_value = apply_term(block, op_one[state_number, 0], op_two[state_number, 0], op_three[state_number, 0])
        diagonal_value = diagonal_value + apply_term(block, op_one[state_number, 1], op_two[state_number, 1], op_three[state_number, 1])
        diagonal_parts.append(diagonal_value)
        coupling_parts.append(apply_term(block, op_one[state_number, 2], op_two[state_number, 2], op_three[state_number, 2]))
    results = []
    for state_number in range(N_STATE):
        combined = diagonal_parts[state_number] + coupling_parts[1 - state_number]
        applied = lax.optimization_barrier(combined.astype(jnp.bfloat16))
        results.append(core[state_number].astype(jnp.float32) - 0.5 * applied.astype(jnp.float32))
    return jnp.stack(results)
```

```python
import functools

import jax
import jax.numpy as jnp
from jax import lax
from jax.experimental import pallas as pl
from jax.experimental.pallas import tpu as pltpu
from jax.sharding import PartitionSpec as P

CHUNK_ROWS = 32
MIB = 1 << 20


def one_two_kernel(outer, terms, step_rows, *refs):
    own_ref = refs[0]
    ups = refs[1 : outer]
    downs = refs[outer : 2 * outer - 1]
    first_ref, third_ref, out_ref = refs[2 * outer - 1 :]
    place = lax.axis_index("mode") // (lax.axis_size("mode") // outer)

    def body(row, carry):
        blocks = [own_ref[row]]
        for hop in range(1, outer):
            blocks.append(
                jnp.where(place >= hop, ups[hop - 1][row], downs[outer - hop - 1][row])
            )
        block = jnp.concatenate(blocks, axis=0) if len(blocks) > 1 else blocks[0]
        for term in range(terms):
            inner = jnp.dot(block, third_ref[term], preferred_element_type=jnp.float32)
            value = jnp.dot(
                first_ref[term], inner.astype(jnp.bfloat16), preferred_element_type=jnp.float32
            )
            out_ref[term, row] = value.astype(jnp.bfloat16)
        return carry

    lax.fori_loop(0, step_rows, body, 0)


def one_three(own, ups, downs, first, third):
    rows, held, depth = own.shape
    terms, made, _ = first.shape
    outer = len(ups) + 1
    step_rows = min(rows, 8)
    piece = pl.BlockSpec((step_rows, held, depth), lambda i: (i, 0, 0))
    whole = lambda shape: pl.BlockSpec(shape, lambda i: (0,) * len(shape))
    flops = 2 * terms * rows * depth * held * outer * (depth + made)
    return pl.pallas_call(
        functools.partial(one_two_kernel, outer, terms, step_rows),
        grid=(rows // step_rows,),
        in_specs=[piece] * (2 * outer - 1) + [whole(first.shape), whole(third.shape)],
        out_specs=pl.BlockSpec((terms, step_rows, made, depth), lambda i: (0, i, 0, 0)),
        out_shape=jax.ShapeDtypeStruct((terms, rows, made, depth), jnp.bfloat16),
        compiler_params=pltpu.CompilerParams(vmem_limit_bytes=48 * MIB),
        cost_estimate=pl.CostEstimate(
            flops=flops,
            bytes_accessed=2 * rows * depth * (held * (2 * outer - 1) + terms * made),
            transcendentals=0,
        ),
        name="third_first",
    )(own, *ups, *downs, first, third)


def final_kernel(pieces, *refs):
    own = refs[:pieces]
    other = refs[pieces : 2 * pieces]
    second_ref, core_ref, out_ref = refs[2 * pieces :]
    for row in range(core_ref.shape[0]):
        parts = [ref[term, row] for term in range(own[0].shape[0]) for ref in own]
        parts += [ref[0, row] for ref in other]
        stacked = jnp.concatenate(parts, axis=0)
        applied = jnp.dot(second_ref[...], stacked, preferred_element_type=jnp.float32)
        out_ref[row] = core_ref[row].astype(jnp.float32) - 0.5 * applied


def final(own, other, second, core):
    rows, count, depth = core.shape
    near = own[0].shape[0]
    chunk = own[0].shape[2]
    step = 2
    flops = 2 * rows * count * second.shape[1] * depth
    return pl.pallas_call(
        functools.partial(final_kernel, len(own)),
        grid=(rows // step,),
        in_specs=[pl.BlockSpec((near, step, chunk, depth), lambda i: (0, i, 0, 0))] * len(own)
        + [pl.BlockSpec((1, step, chunk, depth), lambda i: (0, i, 0, 0))] * len(other)
        + [
            pl.BlockSpec(second.shape, lambda i: (0, 0)),
            pl.BlockSpec((step, count, depth), lambda i: (i, 0, 0)),
        ],
        out_specs=pl.BlockSpec((step, count, depth), lambda i: (i, 0, 0)),
        out_shape=jax.ShapeDtypeStruct((rows, count, depth), jnp.float32),
        compiler_params=pltpu.CompilerParams(vmem_limit_bytes=40 * MIB),
        cost_estimate=pl.CostEstimate(
            flops=flops,
            bytes_accessed=rows * depth * (2 * second.shape[1] + 6 * count),
            transcendentals=0,
        ),
        name="second_final",
    )(*own, *other, second, core)


def shards(core, op_one, op_two, op_three):
    own_core = core[0]
    rows, count, depth = own_core.shape
    terms = op_one.shape[1]
    states = lax.axis_size("state")
    modes = lax.axis_size("mode")
    outer = 4 if modes % 4 == 0 else 1
    inner = modes // outer
    share = count // inner
    chunk = min(share, CHUNK_ROWS)
    state = lax.axis_index("state")
    mode = lax.axis_index("mode")
    place, member = mode // inner, mode % inner

    partner = lambda who, d: who ^ d
    own_first = lax.dynamic_index_in_dim(op_one, state, 0, keepdims=False)
    own_third = lax.dynamic_index_in_dim(op_three, state, 0, keepdims=False)
    own_second = lax.dynamic_index_in_dim(op_two, state, 0, keepdims=False)
    other_second = lax.dynamic_index_in_dim(op_two, states - 1 - state, 0, keepdims=False)

    spot = jnp.arange(modes * rows, dtype=jnp.int32)
    held_place = (place - spot // (inner * rows) + outer) % outer
    held_member = ((spot // rows) % inner) ^ member
    held = (held_place * inner + held_member) * rows + spot % rows
    select = (held[:, None] == spot[None, :]).astype(jnp.bfloat16)
    picked = jnp.einsum("qa,tab->tqb", select[: inner * rows], own_first).astype(jnp.bfloat16)
    first = jnp.einsum("tqb,pb->tqp", picked, select).astype(jnp.bfloat16)
    third = jnp.swapaxes(own_third, 1, 2)

    def columns(matrix):
        return [
            lax.dynamic_slice_in_dim(matrix, partner(member, d) * share, share, 1)
            for d in range(inner)
        ]

    def ordered(matrix):
        return [
            block[:, start : start + chunk]
            for start in range(0, share, chunk)
            for block in columns(matrix)
        ]

    second = []
    for term in range(terms - 1):
        second += ordered(own_second[term])
    second += ordered(other_second[terms - 1])
    second = jnp.concatenate(second, axis=1)

    turned = jnp.swapaxes(own_core, 0, 1)

    def exchange(value, d):
        return lax.ppermute(
            value,
            "mode",
            [
                (z * inner + h, z * inner + partner(h, d))
                for z in range(outer)
                for h in range(inner)
            ],
        )

    def crossed(value, d):
        return lax.ppermute(
            value,
            ("state", "mode"),
            [
                (s * modes + z * inner + h, (states - 1 - s) * modes + z * inner + partner(h, d))
                for s in range(states)
                for z in range(outer)
                for h in range(inner)
            ],
        )

    def relay(value, hop, way):
        pairs = []
        for z in range(outer):
            if 0 <= z + way < outer and 0 <= z - way * (hop - 1) < outer:
                pairs += [(z * inner + h, (z + way) * inner + h) for h in range(inner)]
        return lax.ppermute(value, "mode", pairs)

    near, far = [], []
    for start in range(0, share, chunk):
        pieces = []
        for d in range(inner):
            piece = lax.dynamic_slice_in_dim(turned, partner(member, d) * share + start, chunk, 0)
            pieces.append(exchange(piece, d) if d else piece)
        own = jnp.concatenate(pieces, axis=1)
        ups, downs = [], []
        up = down = own
        for hop in range(1, outer):
            up, down = relay(up, hop, 1), relay(down, hop, -1)
            ups.append(up)
            downs.append(down)
        made = one_three(own, ups, downs, first, third)
        made = made.reshape(terms, chunk, inner, rows, depth)
        for d in range(inner):
            part = jnp.swapaxes(made[:, :, d], 1, 2)
            near.append(exchange(part[:-1], d) if d else part[:-1])
            far.append(crossed(part[-1:], d))
    return final(near, far, second, own_core)[None]


def solution(mesh):
    placed = (P("state", "mode", None, None), P(), P(), P())
    return jax.shard_map(
        shards,
        mesh=mesh,
        in_specs=placed,
        out_specs=P("state", "mode", None, None),
        check_vma=False,
    )
```

```python
import functools

import jax
import jax.numpy as jnp
from jax import lax
from jax.experimental import pallas as pl
from jax.experimental.pallas import tpu as pltpu
from jax.sharding import PartitionSpec as P

CHUNK_ROWS = 16
MIB = 1 << 20


def one_two_kernel(outer, terms, step_rows, *refs):
    own_ref = refs[0]
    ups = refs[1 : outer]
    downs = refs[outer : 2 * outer - 1]
    first_ref, third_ref, out_ref = refs[2 * outer - 1 :]
    made = out_ref.shape[2]
    place = lax.axis_index("mode") // (lax.axis_size("mode") // outer)

    def body(row, carry):
        blocks = [own_ref[row]]
        for hop in range(1, outer):
            blocks.append(
                jnp.where(place >= hop, ups[hop - 1][row], downs[outer - hop - 1][row])
            )
        block = jnp.concatenate(blocks, axis=0) if len(blocks) > 1 else blocks[0]
        mixed = jnp.dot(first_ref[...], block, preferred_element_type=jnp.float32)
        high = mixed.astype(jnp.bfloat16)
        low = (mixed - high.astype(jnp.float32)).astype(jnp.bfloat16)
        for term in range(terms):
            part = slice(term * made, (term + 1) * made)
            matrix = third_ref[term]
            value = jnp.dot(high[part], matrix, preferred_element_type=jnp.float32)
            value += jnp.dot(low[part], matrix, preferred_element_type=jnp.float32)
            out_ref[term, row] = value.astype(jnp.bfloat16)
        return carry

    lax.fori_loop(0, step_rows, body, 0)


def one_three(own, ups, downs, first, third):
    rows, held, depth = own.shape
    terms, made, _ = first.shape
    outer = len(ups) + 1
    step_rows = min(rows, 8)
    piece = pl.BlockSpec((step_rows, held, depth), lambda i: (i, 0, 0))
    whole = lambda shape: pl.BlockSpec(shape, lambda i: (0,) * len(shape))
    flops = 2 * terms * rows * depth * made * (held * outer + 2 * depth)
    stacked = first.reshape(terms * made, first.shape[2])
    return pl.pallas_call(
        functools.partial(one_two_kernel, outer, terms, step_rows),
        grid=(rows // step_rows,),
        in_specs=[piece] * (2 * outer - 1) + [whole(stacked.shape), whole(third.shape)],
        out_specs=pl.BlockSpec((terms, step_rows, made, depth), lambda i: (0, i, 0, 0)),
        out_shape=jax.ShapeDtypeStruct((terms, rows, made, depth), jnp.bfloat16),
        compiler_params=pltpu.CompilerParams(vmem_limit_bytes=48 * MIB),
        cost_estimate=pl.CostEstimate(
            flops=flops,
            bytes_accessed=2 * rows * depth * (held * (2 * outer - 1) + terms * made),
            transcendentals=0,
        ),
        name="third_first",
    )(own, *ups, *downs, stacked, third)


def final_kernel(pieces, *refs):
    own = refs[:pieces]
    other = refs[pieces : 2 * pieces]
    second_ref, core_ref, out_ref = refs[2 * pieces :]
    for row in range(core_ref.shape[0]):
        parts = [ref[term, row] for term in range(own[0].shape[0]) for ref in own]
        parts += [ref[0, row] for ref in other]
        stacked = jnp.concatenate(parts, axis=0)
        applied = jnp.dot(second_ref[...], stacked, preferred_element_type=jnp.float32)
        out_ref[row] = core_ref[row].astype(jnp.float32) - 0.5 * applied


def final(own, other, second, core):
    rows, count, depth = core.shape
    near = own[0].shape[0]
    chunk = own[0].shape[2]
    step = 2
    flops = 2 * rows * count * second.shape[1] * depth
    return pl.pallas_call(
        functools.partial(final_kernel, len(own)),
        grid=(rows // step,),
        in_specs=[pl.BlockSpec((near, step, chunk, depth), lambda i: (0, i, 0, 0))] * len(own)
        + [pl.BlockSpec((1, step, chunk, depth), lambda i: (0, i, 0, 0))] * len(other)
        + [
            pl.BlockSpec(second.shape, lambda i: (0, 0)),
            pl.BlockSpec((step, count, depth), lambda i: (i, 0, 0)),
        ],
        out_specs=pl.BlockSpec((step, count, depth), lambda i: (i, 0, 0)),
        out_shape=jax.ShapeDtypeStruct((rows, count, depth), jnp.float32),
        compiler_params=pltpu.CompilerParams(vmem_limit_bytes=40 * MIB),
        cost_estimate=pl.CostEstimate(
            flops=flops,
            bytes_accessed=rows * depth * (2 * second.shape[1] + 6 * count),
            transcendentals=0,
        ),
        name="second_final",
    )(*own, *other, second, core)


def shards(core, op_one, op_two, op_three):
    own_core = core[0]
    rows, count, depth = own_core.shape
    terms = op_one.shape[1]
    states = lax.axis_size("state")
    modes = lax.axis_size("mode")
    outer = 4 if modes % 4 == 0 else 1
    inner = modes // outer
    share = count // inner
    chunk = min(share, CHUNK_ROWS)
    state = lax.axis_index("state")
    mode = lax.axis_index("mode")
    place, member = mode // inner, mode % inner

    partner = lambda who, d: who ^ d
    own_first = lax.dynamic_index_in_dim(op_one, state, 0, keepdims=False)
    own_third = lax.dynamic_index_in_dim(op_three, state, 0, keepdims=False)
    own_second = lax.dynamic_index_in_dim(op_two, state, 0, keepdims=False)
    other_second = lax.dynamic_index_in_dim(op_two, states - 1 - state, 0, keepdims=False)

    spot = jnp.arange(modes * rows, dtype=jnp.int32)
    held_place = (place - spot // (inner * rows) + outer) % outer
    held_member = ((spot // rows) % inner) ^ member
    held = (held_place * inner + held_member) * rows + spot % rows
    select = (held[:, None] == spot[None, :]).astype(jnp.bfloat16)
    picked = jnp.einsum("qa,tab->tqb", select[: inner * rows], own_first).astype(jnp.bfloat16)
    first = jnp.einsum("tqb,pb->tqp", picked, select).astype(jnp.bfloat16)
    third = jnp.swapaxes(own_third, 1, 2)

    def columns(matrix):
        return [
            lax.dynamic_slice_in_dim(matrix, partner(member, d) * share, share, 1)
            for d in range(inner)
        ]

    second = []
    for term in range(terms - 1):
        second += columns(own_second[term])
    second += columns(other_second[terms - 1])
    second = jnp.concatenate(second, axis=1)

    turned = jnp.swapaxes(own_core, 0, 1)

    def exchange(value, d):
        return lax.ppermute(
            value,
            "mode",
            [
                (z * inner + h, z * inner + partner(h, d))
                for z in range(outer)
                for h in range(inner)
            ],
        )

    def crossed(value, d):
        return lax.ppermute(
            value,
            ("state", "mode"),
            [
                (s * modes + z * inner + h, (states - 1 - s) * modes + z * inner + partner(h, d))
                for s in range(states)
                for z in range(outer)
                for h in range(inner)
            ],
        )

    def relay(value, hop, way):
        pairs = []
        for z in range(outer):
            if 0 <= z + way < outer and 0 <= z - way * (hop - 1) < outer:
                pairs += [(z * inner + h, (z + way) * inner + h) for h in range(inner)]
        return lax.ppermute(value, "mode", pairs)

    def after(*values):
        mark = sum(value[0, 0, 0].astype(jnp.float32) for value in values)
        return (mark * 0.0).astype(jnp.int32)

    near, far, ready, older = [], [], 0, 0
    for start in range(0, share, chunk):
        pieces = []
        for d in range(inner):
            row = partner(member, d) * share + start + ready
            piece = lax.dynamic_slice_in_dim(turned, row, chunk, 0)
            pieces.append(exchange(piece, d) if d else piece)
        own = jnp.concatenate(pieces, axis=1)
        ups, downs = [], []
        up = down = own
        for hop in range(1, outer):
            up, down = relay(up, hop, 1), relay(down, hop, -1)
            ups.append(up)
            downs.append(down)
        if ups:
            ready, older = older, after(ups[1], downs[1])
        made = one_three(own, ups, downs, first, third)
        made = made.reshape(terms, chunk, inner, rows, depth)
        for d in range(inner):
            part = jnp.swapaxes(made[:, :, d], 1, 2)
            near.append(exchange(part[:-1], d) if d else part[:-1])
            far.append(crossed(part[-1:], d))
    by_member = lambda blocks: [block for d in range(inner) for block in blocks[d::inner]]
    return final(by_member(near), by_member(far), second, own_core)[None]


def solution(mesh):
    placed = (P("state", "mode", None, None), P(), P(), P())
    return jax.shard_map(
        shards,
        mesh=mesh,
        in_specs=placed,
        out_specs=P("state", "mode", None, None),
        check_vma=False,
    )
```

```python
import functools

import jax
import jax.numpy as jnp
from jax import lax
from jax.experimental import pallas as pl
from jax.experimental.pallas import tpu as pltpu
from jax.sharding import PartitionSpec as P

CHUNK_ROWS = 32
MIB = 1 << 20


def one_two_kernel(outer, terms, step_rows, *refs):
    own_ref = refs[0]
    ups = refs[1 : outer]
    downs = refs[outer : 2 * outer - 1]
    first_ref, third_ref, out_ref = refs[2 * outer - 1 :]
    made = out_ref.shape[2]
    place = lax.axis_index("mode") // (lax.axis_size("mode") // outer)

    def body(row, carry):
        blocks = [own_ref[row]]
        for hop in range(1, outer):
            blocks.append(
                jnp.where(place >= hop, ups[hop - 1][row], downs[outer - hop - 1][row])
            )
        block = jnp.concatenate(blocks, axis=0) if len(blocks) > 1 else blocks[0]
        mixed = jnp.dot(first_ref[...], block, preferred_element_type=jnp.float32)
        high = mixed.astype(jnp.bfloat16)
        low = (mixed - high.astype(jnp.float32)).astype(jnp.bfloat16)
        for term in range(terms):
            part = slice(term * made, (term + 1) * made)
            matrix = third_ref[term]
            value = jnp.dot(high[part], matrix, preferred_element_type=jnp.float32)
            value += jnp.dot(low[part], matrix, preferred_element_type=jnp.float32)
            out_ref[term, row] = value.astype(jnp.bfloat16)
        return carry

    lax.fori_loop(0, step_rows, body, 0)


def one_three(own, ups, downs, first, third):
    rows, held, depth = own.shape
    terms, made, _ = first.shape
    outer = len(ups) + 1
    step_rows = min(rows, 8)
    piece = pl.BlockSpec((step_rows, held, depth), lambda i: (i, 0, 0))
    whole = lambda shape: pl.BlockSpec(shape, lambda i: (0,) * len(shape))
    flops = 2 * terms * rows * depth * made * (held * outer + 2 * depth)
    stacked = first.reshape(terms * made, first.shape[2])
    return pl.pallas_call(
        functools.partial(one_two_kernel, outer, terms, step_rows),
        grid=(rows // step_rows,),
        in_specs=[piece] * (2 * outer - 1) + [whole(stacked.shape), whole(third.shape)],
        out_specs=pl.BlockSpec((terms, step_rows, made, depth), lambda i: (0, i, 0, 0)),
        out_shape=jax.ShapeDtypeStruct((terms, rows, made, depth), jnp.bfloat16),
        compiler_params=pltpu.CompilerParams(vmem_limit_bytes=48 * MIB),
        cost_estimate=pl.CostEstimate(
            flops=flops,
            bytes_accessed=2 * rows * depth * (held * (2 * outer - 1) + terms * made),
            transcendentals=0,
        ),
        name="third_first",
    )(own, *ups, *downs, stacked, third)


def final_kernel(pieces, *refs):
    own = refs[:pieces]
    other = refs[pieces : 2 * pieces]
    second_ref, core_ref, out_ref = refs[2 * pieces :]
    for row in range(core_ref.shape[0]):
        parts = [ref[term, row] for term in range(own[0].shape[0]) for ref in own]
        parts += [ref[0, row] for ref in other]
        stacked = jnp.concatenate(parts, axis=0)
        applied = jnp.dot(second_ref[...], stacked, preferred_element_type=jnp.float32)
        out_ref[row] = core_ref[row].astype(jnp.float32) - 0.5 * applied


def final(own, other, second, core):
    rows, count, depth = core.shape
    near = own[0].shape[0]
    chunk = own[0].shape[2]
    step = 2
    flops = 2 * rows * count * second.shape[1] * depth
    return pl.pallas_call(
        functools.partial(final_kernel, len(own)),
        grid=(rows // step,),
        in_specs=[pl.BlockSpec((near, step, chunk, depth), lambda i: (0, i, 0, 0))] * len(own)
        + [pl.BlockSpec((1, step, chunk, depth), lambda i: (0, i, 0, 0))] * len(other)
        + [
            pl.BlockSpec(second.shape, lambda i: (0, 0)),
            pl.BlockSpec((step, count, depth), lambda i: (i, 0, 0)),
        ],
        out_specs=pl.BlockSpec((step, count, depth), lambda i: (i, 0, 0)),
        out_shape=jax.ShapeDtypeStruct((rows, count, depth), jnp.float32),
        compiler_params=pltpu.CompilerParams(vmem_limit_bytes=40 * MIB),
        cost_estimate=pl.CostEstimate(
            flops=flops,
            bytes_accessed=rows * depth * (2 * second.shape[1] + 6 * count),
            transcendentals=0,
        ),
        name="second_final",
    )(*own, *other, second, core)


def shards(core, op_one, op_two, op_three):
    own_core = core[0]
    rows, count, depth = own_core.shape
    terms = op_one.shape[1]
    states = lax.axis_size("state")
    modes = lax.axis_size("mode")
    outer = 4 if modes % 4 == 0 else 1
    inner = modes // outer
    share = count // inner
    chunk = min(share, CHUNK_ROWS)
    state = lax.axis_index("state")
    mode = lax.axis_index("mode")
    place, member = mode // inner, mode % inner

    partner = lambda who, d: who ^ d
    own_first = lax.dynamic_index_in_dim(op_one, state, 0, keepdims=False)
    own_third = lax.dynamic_index_in_dim(op_three, state, 0, keepdims=False)
    own_second = lax.dynamic_index_in_dim(op_two, state, 0, keepdims=False)
    other_second = lax.dynamic_index_in_dim(op_two, states - 1 - state, 0, keepdims=False)

    spot = jnp.arange(modes * rows, dtype=jnp.int32)
    held_place = (place - spot // (inner * rows) + outer) % outer
    held_member = ((spot // rows) % inner) ^ member
    held = (held_place * inner + held_member) * rows + spot % rows
    select = (held[:, None] == spot[None, :]).astype(jnp.bfloat16)
    picked = jnp.einsum("qa,tab->tqb", select[: inner * rows], own_first).astype(jnp.bfloat16)
    first = jnp.einsum("tqb,pb->tqp", picked, select).astype(jnp.bfloat16)
    third = jnp.swapaxes(own_third, 1, 2)

    def columns(matrix):
        return [
            lax.dynamic_slice_in_dim(matrix, partner(member, d) * share, share, 1)
            for d in range(inner)
        ]

    second = []
    for term in range(terms - 1):
        second += columns(own_second[term])
    second += columns(other_second[terms - 1])
    second = jnp.concatenate(second, axis=1)

    turned = jnp.swapaxes(own_core, 0, 1)

    def exchange(value, d):
        return lax.ppermute(
            value,
            "mode",
            [
                (z * inner + h, z * inner + partner(h, d))
                for z in range(outer)
                for h in range(inner)
            ],
        )

    def crossed(value, d):
        return lax.ppermute(
            value,
            ("state", "mode"),
            [
                (s * modes + z * inner + h, (states - 1 - s) * modes + z * inner + partner(h, d))
                for s in range(states)
                for z in range(outer)
                for h in range(inner)
            ],
        )

    def relay(value, hop, way):
        pairs = []
        for z in range(outer):
            if 0 <= z + way < outer and 0 <= z - way * (hop - 1) < outer:
                pairs += [(z * inner + h, (z + way) * inner + h) for h in range(inner)]
        return lax.ppermute(value, "mode", pairs)

    def after(*values):
        mark = sum(value[0, 0, 0].astype(jnp.float32) for value in values)
        return (mark * 0.0).astype(jnp.int32)

    near, far, ready, older = [], [], 0, 0
    for start in range(0, share, chunk):
        pieces = []
        for d in range(inner):
            row = partner(member, d) * share + start + ready
            piece = lax.dynamic_slice_in_dim(turned, row, chunk, 0)
            pieces.append(exchange(piece, d) if d else piece)
        own = jnp.concatenate(pieces, axis=1)
        ups, downs = [], []
        up = down = own
        for hop in range(1, outer):
            up, down = relay(up, hop, 1), relay(down, hop, -1)
            ups.append(up)
            downs.append(down)
        if ups:
            ready, older = older, after(ups[1], downs[1])
        made = one_three(own, ups, downs, first, third)
        made = made.reshape(terms, chunk, inner, rows, depth)
        for d in range(inner):
            part = jnp.swapaxes(made[:, :, d], 1, 2)
            near.append(exchange(part[:-1], d) if d else part[:-1])
            far.append(crossed(part[-1:], d))
    by_member = lambda blocks: [block for d in range(inner) for block in blocks[d::inner]]
    return final(by_member(near), by_member(far), second, own_core)[None]


def solution(mesh):
    placed = (P("state", "mode", None, None), P(), P(), P())
    return jax.shard_map(
        shards,
        mesh=mesh,
        in_specs=placed,
        out_specs=P("state", "mode", None, None),
        check_vma=False,
    )
```
